128 devices in a mesh: dp: 8 (over z, x_hi), seq: 16 (over y, x_lo, core).
Axes of the slice: x: 4 (x_hi: 2, x_lo: 2; x = x_hi * 2 + x_lo), y: 4, z: 4, core: 2. Of those that a mesh axis runs over, the one named last changes fastest.
Arguments:
- query_in: bfloat16 [8, 4096, 2048], P('dp', 'seq'), may hold values from -64 to 64
- key_in: bfloat16 [8, 4096, 2048], P('dp', 'seq'), may hold values from -4 to 4
- value_in: bfloat16 [8, 4096, 2048], P('dp', 'seq'), may hold values from -6 to 6
- out_grad: bfloat16 [8, 4096, 2048], P('dp', 'seq'), may hold values from -12 to 12
- out_weight: bfloat16 [2048, 2048], replicated, may hold values from -0.125 to 0.125
Outputs:
- query_grad: bfloat16 [8, 4096, 2048], P('dp', 'seq')
- key_grad: bfloat16 [8, 4096, 2048], P('dp', 'seq')
- value_grad: bfloat16 [8, 4096, 2048], P('dp', 'seq')
- weight_grad: float32 [2048, 2048], P('seq')
The draws below stay inside these ranges and needn't reach their ends.
All inputs are finite; a program needn't handle non-finite values.
Results may differ from the reference program's by a relative error of at most 0.027.
Values may be sent and summed in bfloat16 or wider, within the bound.
A program may use at most 128 MiB of HBM per device.

```python
import math
import jax
import jax.numpy as jnp
from jax import lax

HEAD = 128
DW = 2048
TOK_DEV = 256
HD = 2048
SEQ = 4096
BATCH = 8
LEVELS = 4
N_SEQ = 16


def draw_key_in(key, part):
    key = jax.random.fold_in(key, 7)
    return jax.random.truncated_normal(key, -4.0, 4.0, (BATCH, SEQ, HD), jnp.float32).astype(jnp.bfloat16)


def draw_query_in(key, part):
    key = jax.random.fold_in(key, 11)
    return jax.random.truncated_normal(key, -4.0, 4.0, (BATCH, SEQ, HD), jnp.float32).astype(jnp.bfloat16)


def levels(own_key, extent, shards, least, high):
    factor_of = 1.0
    for position, parts in shards:
        draws = jax.random.uniform(jax.random.fold_in(jax.random.fold_in(own_key, 6), position), (parts,), jnp.float32, least / len(shards), high / len(shards))
        factor_of = factor_of * jnp.repeat(jnp.exp(draws), extent[position] // parts).reshape((-1,) + (1,) * (len(extent) - 1 - position))
    return factor_of


def normal_values(key, extent, width, limit, cuts=(), kind=jnp.bfloat16):
    gain = levels(key, extent, cuts, -0.22, 0.18) if cuts else 1.0
    drawn = jax.random.normal(key, extent, jnp.float32) * width * gain
    return jnp.minimum(jnp.maximum(drawn, -limit), limit).astype(kind)


def setup_inputs(seed: int = 0) -> dict:
    key_list = jax.random.split(jax.random.key(seed), 6)
    query_in = draw_query_in(jax.random.fold_in(key_list[5], 71), 0)
    key_in = draw_key_in(jax.random.fold_in(key_list[5], 71), 0)
    value_in = normal_values(key_list[2], (BATCH, SEQ, HD), 1.0, 6.0, ((0, 8), (1, 16)))
    out_grad = normal_values(key_list[3], (BATCH, SEQ, DW), 2.0, 12.0, ((0, 8), (1, 16)))
    out_weight = normal_values(key_list[4], (HD, DW), HD ** -0.5, 0.125)
    return dict(query_in=query_in, key_in=key_in, value_in=value_in, out_grad=out_grad, out_weight=out_weight)


def attend_head(query_head, key_head, value_head, keep_mask, grad_head, scaling):
    scores = jnp.dot(query_head, key_head.T, preferred_element_type=jnp.float32) * scaling
    scores = jnp.where(keep_mask, scores, -1e+30)
    top_score = lax.optimization_barrier(jnp.max(scores, axis=1, keepdims=True))
    exponent = jnp.where(keep_mask, jnp.exp(scores - top_score), 0.0)
    weights_full = exponent / lax.optimization_barrier(jnp.sum(exponent, axis=1, keepdims=True))
    weights_low = weights_full.astype(jnp.bfloat16)
    attended = jnp.dot(weights_low, value_head, preferred_element_type=jnp.float32).astype(jnp.bfloat16)
    grad_weights = jnp.dot(grad_head, value_head.T, preferred_element_type=jnp.float32)
    inner_sum = lax.optimization_barrier(jnp.sum(weights_full * grad_weights, axis=1, keepdims=True))
    grad_scores = (weights_full * (grad_weights - inner_sum) * scaling).astype(jnp.bfloat16)
    grad_query = jnp.dot(grad_scores, key_head, preferred_element_type=jnp.float32)
    grad_key = jnp.dot(grad_scores.T, query_head, preferred_element_type=jnp.float32)
    grad_value = jnp.dot(weights_low.T, grad_head, preferred_element_type=jnp.float32)
    return (attended, grad_query, grad_key, grad_value)

def sequence_head(query_seq, key_seq, value_seq, grad_seq):
    blocks = N_SEQ
    scaling = 1.0 / math.sqrt(HEAD)
    strides = [2 ** level for level in range(LEVELS)]

    def to_blocks(whole):
        return whole.reshape(blocks, TOK_DEV, HEAD)
    key_blocks = to_blocks(key_seq)
    value_blocks = to_blocks(value_seq)
    key_parts = [key_blocks]
    value_parts = [value_blocks]
    causal = jnp.tril(jnp.ones((TOK_DEV, TOK_DEV), dtype=bool))
    mask_parts = [jnp.broadcast_to(causal, (blocks, TOK_DEV, TOK_DEV))]
    block_ids = jnp.arange(blocks)
    for stride in strides:

        def earlier(whole):
            padding = jnp.zeros((stride, TOK_DEV, HEAD), whole.dtype)
            return jnp.concatenate([padding, whole[:-stride]], axis=0)[:, ::stride]
        key_parts.append(earlier(key_blocks))
        value_parts.append(earlier(value_blocks))
        mask_parts.append(jnp.broadcast_to((block_ids >= stride)[:, None, None], (blocks, TOK_DEV, TOK_DEV // stride)))
    key_all = jnp.concatenate(key_parts, axis=1)
    value_all = jnp.concatenate(value_parts, axis=1)
    keep_mask = jnp.concatenate(mask_parts, axis=2)
    attended, grad_query, grad_key, grad_value = jax.vmap(attend_head, in_axes=(0, 0, 0, 0, 0, None))(to_blocks(query_seq), key_all, value_all, keep_mask, to_blocks(grad_seq), scaling)
    paired = jnp.stack([grad_key, grad_value])
    total = paired[:, :, :TOK_DEV]
    offset = TOK_DEV
    for stride in strides:
        amount = TOK_DEV // stride
        piece = paired[:, :, offset:offset + amount]
        offset = offset + amount
        padding = jnp.zeros((2, stride, amount, HEAD), piece.dtype)
        back = jnp.concatenate([piece[:, stride:], padding], axis=1).astype(jnp.bfloat16)
        back = lax.optimization_barrier(back).astype(jnp.float32)
        total = total.reshape(2, blocks, amount, stride, HEAD).at[:, :, :, 0].add(back).reshape(2, blocks, TOK_DEV, HEAD)
    return (attended.reshape(SEQ, HEAD), grad_query.reshape(SEQ, HEAD).astype(jnp.bfloat16), total[0].reshape(SEQ, HEAD).astype(jnp.bfloat16), total[1].reshape(SEQ, HEAD).astype(jnp.bfloat16))

def reference(query_in, key_in, value_in, out_grad, out_weight):
    grad_attn = jnp.dot(out_grad.reshape(-1, DW), out_weight.T, preferred_element_type=jnp.float32)
    grad_attn = grad_attn.astype(jnp.bfloat16).reshape(BATCH, SEQ, HD)

    def split_heads(whole):
        return whole.reshape(SEQ, HD // HEAD, HEAD).transpose(1, 0, 2)

    def join_heads(stacked):
        return stacked.transpose(1, 0, 2).reshape(SEQ, HD)

    def one_sequence(operands):
        results = lax.map(lambda group: sequence_head(*group), tuple((split_heads(member) for member in operands)))
        return tuple((join_heads(member) for member in results))
    attended, query_grad, key_grad, value_grad = lax.map(one_sequence, (query_in, key_in, value_in, grad_attn))
    weight_grad = lax.dot_general(attended.reshape(-1, HD), out_grad.reshape(-1, DW), (((0,), (0,)), ((), ())), preferred_element_type=jnp.float32)
    return (query_grad, key_grad, value_grad, weight_grad)
```

```python
import functools
import math

import jax
import jax.numpy as jnp
from jax import lax
from jax.experimental import pallas as pl
from jax.experimental.pallas import tpu as pltpu
from jax.sharding import PartitionSpec as P

HEAD = 128
TOK = 256
GROUPS = 8
GW = 256
KEYS = 768
ROWS = (256, 128, 64, 32)
OFFS = (256, 512, 640, 704)
NSEQ = 16
NDP = 8
AHEAD = 3
MESH = pl.DeviceIdType.MESH
F32 = jnp.float32
BF16 = jnp.bfloat16


def dot(a, b, ca, cb):
    return lax.dot_general(a, b, (((ca,), (cb,)), ((), ())), preferred_element_type=F32)


def row_of(p):
    return jnp.where(
        p < 32,
        8 * p,
        jnp.where(
            p < 64, 8 * (p - 32) + 4, jnp.where(p < 128, 4 * (p - 64) + 2, 2 * (p - 128) + 1)
        ),
    )


def kernel(
    q_hbm, k_hbm, v_hbm, og_hbm, w_hbm,
    dq_hbm, dk_hbm, dv_hbm, wg_hbm,
    q_v, raw, og2, w_v, kvp, par, relay, ret, acc, att_own, att_out, att_in,
    zs, zr, ys, yr, xs, xr, wgp, dq_st, dkv_st, wg_st, bias, pm, pmt,
    ld, fs, fr, bs, br, ats, atr, ogs, zss, zrs, yss, yrs, xss, xrs, gss, grs, outs,
):
    scaling = 1.0 / math.sqrt(HEAD)
    factor = scaling * math.log2(math.e)
    dp, c = lax.axis_index("dp"), lax.axis_index("seq")
    z, xh = dp // 2, dp % 2
    y, xl, core = c // 4, (c // 2) % 2, c % 2
    even, odd = core == 0, core == 1
    sibling = c + 1 - 2 * core

    def remote(src, dst, ss, rs, to_dp, to_c):
        return pltpu.make_async_remote_copy(
            src_ref=src, dst_ref=dst, send_sem=ss, recv_sem=rs,
            device_id=(to_dp, to_c), device_id_type=MESH,
        )

    def load_kv(g, which):
        src = (k_hbm, v_hbm)[which]
        return pltpu.make_async_copy(
            src.at[0, :, pl.ds(g * GW, GW)], raw.at[g, :, pl.ds(which * GW, GW)], ld.at[g, which]
        )

    def load_q(g):
        return pltpu.make_async_copy(q_hbm.at[0, :, pl.ds(g * GW, GW)], q_v.at[g], ld.at[g, 2])

    def load_w(g):
        return pltpu.make_async_copy(w_hbm.at[pl.ds(g * GW, GW)], w_v.at[g], ld.at[g, 3])

    load_og = pltpu.make_async_copy(og_hbm.at[0], og2.at[0], ld.at[GROUPS, 0])

    partners = (
        [(dp, (c + d) % NSEQ) for d in (1, 15, 2, 14, 4, 8, 12)]
        + [((dp + d) % NDP, c) for d in range(1, NDP)]
        + [(dp + 1 - 2 * xh, c + 2 - 4 * xl)]
    )
    barrier = pltpu.get_barrier_semaphore()
    for partner in partners:
        pl.semaphore_signal(barrier, inc=1, device_id=partner, device_id_type=MESH)
    for g in range(GROUPS):
        load_kv(g, 0).start()
        load_kv(g, 1).start()
        if g == 0:
            load_og.start()
        load_q(g).start()
        load_w(g).start()

    pos0 = lax.broadcasted_iota(jnp.int32, (TOK, TOK), 0)
    pos1 = lax.broadcasted_iota(jnp.int32, (TOK, TOK), 1)
    pm[...] = (row_of(pos0) == pos1).astype(F32).astype(BF16)
    pmt[...] = (row_of(pos1) == pos0).astype(F32).astype(BF16)
    bias[0:TOK] = jnp.where(row_of(pos0) <= pos1, 0.0, -1e30).astype(F32)
    for level in range(4):
        shown = jnp.where(c >= 2**level, 0.0, -1e30).astype(F32)
        bias[pl.ds(OFFS[level], ROWS[level])] = jnp.full((ROWS[level], TOK), shown, F32)

        @pl.when(c < 2**level)
        def _():
            for g in range(GROUPS):
                kvp[g, pl.ds(OFFS[level], ROWS[level])] = jnp.zeros((ROWS[level], 2 * GW), BF16)

    bias[pl.ds(736, 32)] = jnp.full((32, TOK), -1e30, F32)
    for g in range(GROUPS):
        kvp[g, pl.ds(736, 32)] = jnp.zeros((32, 2 * GW), BF16)

    def fwd(g, level):
        return remote(
            kvp.at[g, pl.ds(0, ROWS[level])], kvp.at[g, pl.ds(OFFS[level], ROWS[level])],
            fs.at[g, level], fr.at[g, level], dp, (c + 2**level) % NSEQ,
        )

    def fwd_on(g):
        return remote(
            kvp.at[g, pl.ds(OFFS[0], ROWS[1])], kvp.at[g, pl.ds(OFFS[1], ROWS[1])],
            fs.at[g, 4], fr.at[g, 1], dp, sibling,
        )

    sends = (c < 15, jnp.logical_and(even, c < 14), c < 12, c < 8)
    takes = (c >= 1, c >= 2, c >= 4, c >= 8)
    hands_on = jnp.logical_and(even, c >= 2)

    def send_halos(g):
        load_kv(g, 0).wait()
        load_kv(g, 1).wait()
        kvp[g, pl.ds(0, TOK)] = dot(pm[...], raw[g], 1, 0).astype(BF16)
        for level in range(4):

            @pl.when(sends[level])
            def _():
                fwd(g, level).start()

    def bwd(g, level):
        return remote(
            par.at[g, pl.ds(OFFS[level] - TOK, ROWS[level])],
            ret.at[g, pl.ds(OFFS[level] - TOK, ROWS[level])],
            bs.at[g, level], br.at[g, level], dp, (c - 2**level + NSEQ) % NSEQ,
        )

    def bwd_relay(g):
        return remote(
            par.at[g, pl.ds(OFFS[1] - TOK, ROWS[1])], relay.at[g],
            bs.at[g, 1], br.at[g, 4], dp, sibling,
        )

    def send_back(g):
        @pl.when(odd)
        def _():
            bwd(g, 0).start()

        @pl.when(jnp.logical_and(odd, c >= 3))
        def _():
            bwd_relay(g).start()

        @pl.when(hands_on)
        def _():
            bwd(g, 1).start()

        @pl.when(c >= 4)
        def _():
            bwd(g, 2).start()

        @pl.when(c >= 8)
        def _():
            bwd(g, 3).start()

    def merge_back(g):
        @pl.when(hands_on)
        def _():
            bwd_relay(g).wait_recv()
            merged = par[g, pl.ds(0, ROWS[1])].astype(F32) + relay[g].astype(F32)
            par[g, pl.ds(0, ROWS[1])] = merged.astype(BF16)
            bwd(g, 0).start()

    comes_back = (c < 15, jnp.logical_and(even, c < 14), c < 12, c < 8)

    def store_kv(g, which):
        dst = (dk_hbm, dv_hbm)[which]
        return pltpu.make_async_copy(
            dkv_st.at[g, :, pl.ds(which * GW, GW)],
            dst.at[0, :, pl.ds(pl.multiple_of(g * GW, GW), GW)],
            outs.at[g, which],
        )

    def store_q(g):
        return pltpu.make_async_copy(
            dq_st.at[g], dq_hbm.at[0, :, pl.ds(pl.multiple_of(g * GW, GW), GW)], outs.at[g, 2]
        )

    def finish_kv(g):
        for level in range(4):

            @pl.when(comes_back[level])
            def _():
                bwd(g, level).wait_recv()
                acc[g, pl.ds(0, ROWS[level])] += ret[
                    g, pl.ds(OFFS[level] - TOK, ROWS[level])
                ].astype(F32)

        dkv_st[g] = dot(pmt[...], acc[g].astype(BF16), 1, 0).astype(BF16)
        store_kv(g, 0).start()
        store_kv(g, 1).start()

    def att_send(g):
        return remote(att_out.at[g], att_in.at[g], ats.at[g], atr.at[g], dp, sibling)

    og_send = remote(og2.at[0], og2.at[1], ogs.at[0], ogs.at[1], dp, sibling)

    def z_send(g, k):
        to = (z + k) % 4
        return remote(
            zs.at[g, to], zr.at[g, k - 1], zss.at[g, k - 1], zrs.at[g, k - 1], to * 2 + xh, c
        )

    def weight_terms(g):
        att_send(g).wait_recv()
        for part in range(4):
            cols = pl.ds(part * 512, 512)
            terms = dot(att_own[g], og2[0, :, cols], 1, 0) + dot(att_in[g], og2[1, :, cols], 1, 0)
            zs[g, part] = terms.astype(BF16)
        for k in (1, 2, 3):
            z_send(g, k).start()

    def y_send(g):
        k = (g // 2 - y + 4) % 4
        return remote(
            ys.at[g], yr.at[g % 2, k - 1], yss.at[g], yrs.at[g % 2, k - 1],
            dp, (g // 2) * 4 + c % 4,
        )

    def z_sum(g):
        total = zs[g, z].astype(F32)
        for k in (1, 2, 3):
            z_send(g, k).wait_recv()
        for k in (1, 2, 3):
            total = total + zr[g, k - 1].astype(F32)
        ys[g] = total.astype(BF16)

        @pl.when(g // 2 != y)
        def _():
            y_send(g).start()

    def x_send(j, half):
        k = (half * 2 + j - (xh * 2 + xl) + 4) % 4
        return k, remote(
            xs.at[j, half], xr.at[k - 1], xss.at[j * 2 + half], xrs.at[k - 1],
            z * 2 + half, y * 4 + j * 2 + core,
        )

    def y_sum():
        for j in (0, 1):
            total = ys[2 * y + j].astype(F32)
            for k in (1, 2, 3):
                remote(
                    yr.at[j, k - 1], yr.at[j, k - 1], yss.at[0], yrs.at[j, k - 1], dp, sibling
                ).wait_recv()
                total = total + yr[j, k - 1].astype(F32)
            for half in (0, 1):
                xs[j, half] = total[:, half * 256 : half * 256 + 256].astype(BF16)
                k, copy = x_send(j, half)

                @pl.when(k != 0)
                def _():
                    copy.start()

    def share(k):
        return remote(
            wgp.at[dp], wgp.at[dp], gss.at[k - 1], grs.at[k - 1], (dp + k) % NDP, c
        )

    def x_sum():
        total = xs[xl, xh].astype(F32)
        for k in (1, 2, 3):
            remote(xr.at[k - 1], xr.at[k - 1], xss.at[0], xrs.at[k - 1], dp, sibling).wait_recv()
            total = total + xr[k - 1].astype(F32)
        wgp[dp] = total.astype(BF16)
        for k in range(1, NDP):
            share(k).start()

    def group(g):
        load_q(g).wait()
        load_w(g).wait()
        grad_attn = dot(og2[0], w_v[g], 1, 1).astype(BF16)
        for hh in (0, 1):
            kcols = pl.ds(hh * HEAD, HEAD)
            vcols = pl.ds(GW + hh * HEAD, HEAD)
            keys, values = kvp[g, :, kcols], kvp[g, :, vcols]
            query = q_v[g, :, kcols]
            grad = grad_attn[:, hh * HEAD : (hh + 1) * HEAD]
            scores = dot(keys, query, 1, 1) + bias[...]
            top = jnp.max(scores, axis=0, keepdims=True)
            expo = jnp.exp2((scores - top) * factor)
            probs = expo * (1.0 / jnp.sum(expo, axis=0, keepdims=True))
            low = probs.astype(BF16)
            dprobs = dot(values, grad, 1, 1)
            inner = jnp.sum(probs * dprobs, axis=0, keepdims=True)
            dscores = (probs * (dprobs - inner)).astype(BF16)
            attended = dot(values, low, 0, 0).astype(BF16)

            @pl.when(core == hh)
            def _():
                att_own[g] = attended

            @pl.when(core != hh)
            def _():
                att_out[g] = attended

            grad_q = dot(keys, dscores, 0, 0) * scaling
            dq_st[g, :, kcols] = grad_q.T.astype(BF16)
            grad_k = dot(dscores, query, 1, 0) * scaling
            grad_v = dot(low, grad, 1, 0)
            acc[g, :, kcols] = grad_k[0:TOK]
            acc[g, :, vcols] = grad_v[0:TOK]
            par[g, :, kcols] = grad_k[TOK:736].astype(BF16)
            par[g, :, vcols] = grad_v[TOK:736].astype(BF16)

    pl.semaphore_wait(barrier, len(partners))
    for g in range(AHEAD):
        send_halos(g)
    load_og.wait()
    og_send.start()

    def step(g, carry):
        for level in range(4):

            @pl.when(takes[level])
            def _():
                fwd(g, level).wait_recv()

            if level == 0:

                @pl.when(hands_on)
                def _():
                    fwd_on(g).start()

        @pl.when(g + AHEAD < GROUPS)
        def _():
            send_halos(g + AHEAD)

        group(g)
        att_send(g).start()
        store_q(g).start()
        send_back(g)

        @pl.when(g >= 1)
        def _():
            merge_back(g - 1)

            @pl.when(g == 1)
            def _():
                og_send.wait_recv()

            weight_terms(g - 1)

        @pl.when(g >= 3)
        def _():
            z_sum(g - 3)

        return carry

    lax.fori_loop(0, GROUPS, step, 0)
    merge_back(GROUPS - 1)
    weight_terms(GROUPS - 1)

    def tail(g, carry):
        finish_kv(g)

        @pl.when(g < 3)
        def _():
            z_sum(g + GROUPS - 3)

        @pl.when(g == 4)
        def _():
            y_sum()

        @pl.when(g == 5)
        def _():
            x_sum()

        return carry

    lax.fori_loop(0, GROUPS, tail, 0)
    for k in range(1, NDP):
        come = wgp.at[(dp - k + NDP) % NDP]
        remote(come, come, gss.at[0], grs.at[k - 1], dp, sibling).wait_recv()
    for part in range(NDP):
        wg_st[:, pl.ds(part * 256, 256)] = wgp[part].astype(F32)
    wg_store = pltpu.make_async_copy(wg_st, wg_hbm, outs.at[GROUPS, 0])
    wg_store.start()

    og_send.wait_send()

    def drain(g, carry):
        store_q(g).wait()
        store_kv(g, 0).wait()
        store_kv(g, 1).wait()
        att_send(g).wait_send()
        for k in (1, 2, 3):
            z_send(g, k).wait_send()

        @pl.when(g // 2 != y)
        def _():
            y_send(g).wait_send()

        for level in range(4):

            @pl.when(sends[level])
            def _():
                fwd(g, level).wait_send()

        @pl.when(hands_on)
        def _():
            fwd_on(g).wait_send()
            bwd(g, 1).wait_send()

        @pl.when(c >= 1)
        def _():
            bwd(g, 0).wait_send()

        @pl.when(jnp.logical_and(odd, c >= 3))
        def _():
            bwd_relay(g).wait_send()

        @pl.when(c >= 4)
        def _():
            bwd(g, 2).wait_send()

        @pl.when(c >= 8)
        def _():
            bwd(g, 3).wait_send()

        return carry

    lax.fori_loop(0, GROUPS, drain, 0)
    for j in (0, 1):
        for half in (0, 1):
            k, copy = x_send(j, half)

            @pl.when(k != 0)
            def _():
                copy.wait_send()

    for k in range(1, NDP):
        share(k).wait_send()
    wg_store.wait()


def per_device(query_in, key_in, value_in, out_grad, out_weight):
    vm = pltpu.VMEM
    dma = pltpu.SemaphoreType.DMA
    g = GROUPS
    return pl.pallas_call(
        kernel,
        out_shape=(
            jax.ShapeDtypeStruct((1, TOK, 2048), BF16),
            jax.ShapeDtypeStruct((1, TOK, 2048), BF16),
            jax.ShapeDtypeStruct((1, TOK, 2048), BF16),
            jax.ShapeDtypeStruct((128, 2048), F32),
        ),
        in_specs=[pl.BlockSpec(memory_space=pl.ANY)] * 5,
        out_specs=(pl.BlockSpec(memory_space=pl.ANY),) * 4,
        scratch_shapes=[
            vm((g, TOK, GW), BF16),
            vm((g, TOK, 2 * GW), BF16),
            vm((2, TOK, 2048), BF16),
            vm((g, GW, 2048), BF16),
            vm((g, KEYS, 2 * GW), BF16),
            vm((g, 480, 2 * GW), BF16),
            vm((g, 128, 2 * GW), BF16),
            vm((g, 480, 2 * GW), BF16),
            vm((g, TOK, 2 * GW), F32),
            vm((g, HEAD, TOK), BF16),
            vm((g, HEAD, TOK), BF16),
            vm((g, HEAD, TOK), BF16),
            vm((g, 4, HEAD, 512), BF16),
            vm((g, 3, HEAD, 512), BF16),
            vm((g, HEAD, 512), BF16),
            vm((2, 3, HEAD, 512), BF16),
            vm((2, 2, HEAD, 256), BF16),
            vm((3, HEAD, 256), BF16),
            vm((NDP, HEAD, 256), BF16),
            vm((g, TOK, GW), BF16),
            vm((g, TOK, 2 * GW), BF16),
            vm((HEAD, 2048), F32),
            vm((KEYS, TOK), F32),
            vm((TOK, TOK), BF16),
            vm((TOK, TOK), BF16),
            dma((g + 1, 4)),
            dma((g, 5)),
            dma((g, 5)),
            dma((g, 5)),
            dma((g, 5)),
            dma((g,)),
            dma((g,)),
            dma((2,)),
            dma((g, 3)),
            dma((g, 3)),
            dma((g,)),
            dma((2, 3)),
            dma((4,)),
            dma((3,)),
            dma((NDP - 1,)),
            dma((NDP - 1,)),
            dma((g + 1, 3)),
        ],
        compiler_params=pltpu.CompilerParams(
            collective_id=0, has_side_effects=True, vmem_limit_bytes=60 * 2**20
        ),
        name="logsparse_backward",
    )(query_in, key_in, value_in, out_grad, out_weight)


def solution(mesh):
    return jax.shard_map(
        per_device,
        mesh=mesh,
        in_specs=(
            P("dp", "seq", None),
            P("dp", "seq", None),
            P("dp", "seq", None),
            P("dp", "seq", None),
            P(),
        ),
        out_specs=(
            P("dp", "seq", None),
            P("dp", "seq", None),
            P("dp", "seq", None),
            P("seq", None),
        ),
        check_vma=False,
    )
```

```python
import functools
import math

import jax
import jax.numpy as jnp
from jax import lax
from jax.experimental import pallas as pl
from jax.experimental.pallas import tpu as pltpu
from jax.sharding import PartitionSpec as P

HEAD = 128
TOK = 256
GROUPS = 8
GW = 256
KEYS = 768
ROWS = (256, 128, 64, 32)
OFFS = (256, 512, 640, 704)
NSEQ = 16
NDP = 8
AHEAD = 3
HOPS_B = 6
MESH = pl.DeviceIdType.MESH
F32 = jnp.float32
BF16 = jnp.bfloat16


def dot(a, b, ca, cb):
    return lax.dot_general(a, b, (((ca,), (cb,)), ((), ())), preferred_element_type=F32)


def cols_of(g):
    return pl.ds(pl.multiple_of(((g % 4) * 2 + g // 4) * GW, GW), GW)


def row_of(p):
    return jnp.where(
        p < 32,
        8 * p,
        jnp.where(
            p < 64, 8 * (p - 32) + 4, jnp.where(p < 128, 4 * (p - 64) + 2, 2 * (p - 128) + 1)
        ),
    )


def kernel(
    q_hbm, k_hbm, v_hbm, og_hbm, w_hbm,
    dq_hbm, dk_hbm, dv_hbm, wg_hbm,
    q_v, raw, og2, w_v, kvp, par, relay, ret, acc, hop_f, hop_b, att_own, att_out, att_in,
    zs, zr, ys, yr, xs, xr, wgp, dq_st, dkv_st, wg_st, bias, pm, pmt,
    ld, fs, fr, bs, br, ats, atr, ogs, zss, zrs, yss, yrs, xss, xrs, gss, grs, outs,
):
    scaling = 1.0 / math.sqrt(HEAD)
    factor = scaling * math.log2(math.e)
    dp, c = lax.axis_index("dp"), lax.axis_index("seq")
    z, xh = dp // 2, dp % 2
    y, xl, core = c // 4, (c // 2) % 2, c % 2
    even, odd = core == 0, core == 1
    sibling = c + 1 - 2 * core

    def remote(src, dst, ss, rs, to_dp, to_c):
        return pltpu.make_async_remote_copy(
            src_ref=src, dst_ref=dst, send_sem=ss, recv_sem=rs,
            device_id=(to_dp, to_c), device_id_type=MESH,
        )

    def load_kv(g, which):
        src = (k_hbm, v_hbm)[which]
        return pltpu.make_async_copy(
            src.at[0, :, cols_of(g)], raw.at[g, :, pl.ds(which * GW, GW)], ld.at[g, which]
        )

    def load_q(g):
        return pltpu.make_async_copy(q_hbm.at[0, :, cols_of(g)], q_v.at[g], ld.at[g, 2])

    def load_w(g):
        return pltpu.make_async_copy(w_hbm.at[cols_of(g)], w_v.at[g], ld.at[g, 3])

    load_og = pltpu.make_async_copy(og_hbm.at[0], og2.at[0], ld.at[GROUPS, 0])

    partners = (
        [(dp, (c + d) % NSEQ) for d in (1, 15, 2, 14, 3, 13, 4, 8, 12)]
        + [((dp + d) % NDP, c) for d in range(1, NDP)]
        + [(dp + 1 - 2 * xh, c + 2 - 4 * xl)]
    )
    barrier = pltpu.get_barrier_semaphore()
    for partner in partners:
        pl.semaphore_signal(barrier, inc=1, device_id=partner, device_id_type=MESH)
    for g in range(GROUPS):
        load_kv(g, 0).start()
        load_kv(g, 1).start()
        if g == 0:
            load_og.start()
        load_q(g).start()
        load_w(g).start()

    pos0 = lax.broadcasted_iota(jnp.int32, (TOK, TOK), 0)
    pos1 = lax.broadcasted_iota(jnp.int32, (TOK, TOK), 1)
    pm[...] = (row_of(pos0) == pos1).astype(F32).astype(BF16)
    pmt[...] = (row_of(pos1) == pos0).astype(F32).astype(BF16)
    bias[0:TOK] = jnp.where(row_of(pos0) <= pos1, 0.0, -1e30).astype(F32)
    for level in range(4):
        shown = jnp.where(c >= 2**level, 0.0, -1e30).astype(F32)
        bias[pl.ds(OFFS[level], ROWS[level])] = jnp.full((ROWS[level], TOK), shown, F32)

        @pl.when(c < 2**level)
        def _():
            for g in range(GROUPS):
                kvp[g, pl.ds(OFFS[level], ROWS[level])] = jnp.zeros((ROWS[level], 2 * GW), BF16)

    bias[pl.ds(736, 32)] = jnp.full((32, TOK), -1e30, F32)
    for g in range(GROUPS):
        kvp[g, pl.ds(736, 32)] = jnp.zeros((32, 2 * GW), BF16)

    def fwd(g, level):
        return remote(
            kvp.at[g, pl.ds(0, ROWS[level])], kvp.at[g, pl.ds(OFFS[level], ROWS[level])],
            fs.at[g, level], fr.at[g, level], dp, (c + 2**level) % NSEQ,
        )

    def fwd_on(g):
        return remote(
            kvp.at[g, pl.ds(OFFS[0], ROWS[1])], kvp.at[g, pl.ds(OFFS[1], ROWS[1])],
            fs.at[g, 4], fr.at[g, 1], dp, sibling,
        )

    sends = (c < 15, jnp.logical_and(even, c < 14), c < 12, c < 8)
    takes = (c >= 1, c >= 2, c >= 4, c >= 8)
    hands_on = jnp.logical_and(even, c >= 2)

    turns_f = jnp.logical_and(c % 4 == 3, c < 15)
    hops_f = jnp.logical_and(c % 4 == 3, c >= 7)

    def fwd_turn(g):
        return remote(
            kvp.at[g, pl.ds(0, TOK)], hop_f.at[g], fs.at[g, 0], fr.at[g, 4], dp, (c + 4) % NSEQ
        )

    def fwd_hop(g):
        return remote(
            hop_f.at[g], kvp.at[g, pl.ds(OFFS[0], TOK)], fs.at[g, 4], fr.at[g, 0],
            dp, (c - 3 + NSEQ) % NSEQ,
        )

    def hop_on(g):
        @pl.when(hops_f)
        def _():
            fwd_turn(g).wait_recv()
            fwd_hop(g).start()

    def send_level1(g):
        @pl.when(sends[1])
        def _():
            fwd(g, 1).start()

    def send_halos(g):
        load_kv(g, 0).wait()
        load_kv(g, 1).wait()
        kvp[g, pl.ds(0, TOK)] = dot(pm[...], raw[g], 1, 0).astype(BF16)

        @pl.when(turns_f)
        def _():
            fwd_turn(g).start()

        @pl.when(jnp.logical_and(c % 4 != 3, sends[0]))
        def _():
            fwd(g, 0).start()

        for level in (2, 3):

            @pl.when(sends[level])
            def _():
                fwd(g, level).start()

    def bwd(g, level):
        return remote(
            par.at[g, pl.ds(OFFS[level] - TOK, ROWS[level])],
            ret.at[g, pl.ds(OFFS[level] - TOK, ROWS[level])],
            bs.at[g, level], br.at[g, level], dp, (c - 2**level + NSEQ) % NSEQ,
        )

    def bwd_relay(g):
        return remote(
            par.at[g, pl.ds(OFFS[1] - TOK, ROWS[1])], relay.at[g],
            bs.at[g, 1], br.at[g, 4], dp, sibling,
        )

    def turns_b(g):
        return jnp.logical_and(jnp.logical_and(c % 4 == 0, c >= 4), g < HOPS_B)

    def bwd_turn(g):
        return remote(
            par.at[g, pl.ds(0, TOK)], hop_b.at[g], bs.at[g, 0], br.at[g, 5],
            dp, (c - 4 + NSEQ) % NSEQ,
        )

    def bwd_hop(g):
        return remote(
            hop_b.at[g], ret.at[g, pl.ds(0, TOK)], bs.at[g, 5], br.at[g, 0], dp, (c + 3) % NSEQ
        )

    def send_back(g):
        @pl.when(odd)
        def _():
            bwd(g, 0).start()

        @pl.when(jnp.logical_and(odd, c >= 3))
        def _():
            bwd_relay(g).start()

        @pl.when(hands_on)
        def _():
            bwd(g, 1).start()

        @pl.when(c >= 4)
        def _():
            bwd(g, 2).start()

        @pl.when(c >= 8)
        def _():
            bwd(g, 3).start()

    def merge_back(g):
        @pl.when(hands_on)
        def _():
            bwd_relay(g).wait_recv()
            merged = par[g, pl.ds(0, ROWS[1])].astype(F32) + relay[g].astype(F32)
            par[g, pl.ds(0, ROWS[1])] = merged.astype(BF16)

            @pl.when(turns_b(g))
            def _():
                bwd_turn(g).start()

            @pl.when(jnp.logical_not(turns_b(g)))
            def _():
                bwd(g, 0).start()

    def hop_back(g):
        @pl.when(jnp.logical_and(c % 4 == 0, c <= 8))
        def _():
            bwd_turn(g).wait_recv()
            bwd_hop(g).start()

    comes_back = (c < 15, jnp.logical_and(even, c < 14), c < 12, c < 8)

    def store_kv(g, which):
        dst = (dk_hbm, dv_hbm)[which]
        return pltpu.make_async_copy(
            dkv_st.at[g, :, pl.ds(which * GW, GW)],
            dst.at[0, :, cols_of(g)],
            outs.at[g, which],
        )

    def store_q(g):
        return pltpu.make_async_copy(
            dq_st.at[g], dq_hbm.at[0, :, cols_of(g)], outs.at[g, 2]
        )

    def finish_kv(g):
        for level in range(4):

            @pl.when(comes_back[level])
            def _():
                bwd(g, level).wait_recv()
                acc[g, pl.ds(0, ROWS[level])] += ret[
                    g, pl.ds(OFFS[level] - TOK, ROWS[level])
                ].astype(F32)

        dkv_st[g] = dot(pmt[...], acc[g].astype(BF16), 1, 0).astype(BF16)
        store_kv(g, 0).start()
        store_kv(g, 1).start()

    def att_send(g):
        return remote(att_out.at[g], att_in.at[g], ats.at[g], atr.at[g], dp, sibling)

    og_send = remote(og2.at[0], og2.at[1], ogs.at[0], ogs.at[1], dp, sibling)

    def z_send(g, k):
        to = (z + k) % 4
        return remote(
            zs.at[g, to], zr.at[g, k - 1], zss.at[g, k - 1], zrs.at[g, k - 1], to * 2 + xh, c
        )

    def weight_terms(g):
        att_send(g).wait_recv()
        for part in range(4):
            cols = pl.ds(part * 512, 512)
            terms = dot(att_own[g], og2[0, :, cols], 1, 0) + dot(att_in[g], og2[1, :, cols], 1, 0)
            zs[g, part] = terms.astype(BF16)
        for k in (1, 2, 3):
            z_send(g, k).start()

    def y_send(g):
        k = (g % 4 - y + 4) % 4
        return remote(
            ys.at[g], yr.at[g // 4, k - 1], yss.at[g], yrs.at[g // 4, k - 1],
            dp, (g % 4) * 4 + c % 4,
        )

    def z_sum(g):
        total = zs[g, z].astype(F32)
        for k in (1, 2, 3):
            z_send(g, k).wait_recv()
        for k in (1, 2, 3):
            total = total + zr[g, k - 1].astype(F32)
        ys[g] = total.astype(BF16)

        @pl.when(g % 4 != y)
        def _():
            y_send(g).start()

    def x_send(j, half):
        k = (half * 2 + j - (xh * 2 + xl) + 4) % 4
        return k, remote(
            xs.at[j, half], xr.at[k - 1], xss.at[j * 2 + half], xrs.at[k - 1],
            z * 2 + half, y * 4 + j * 2 + core,
        )

    def y_sum():
        for j in (0, 1):
            total = ys[y + 4 * j].astype(F32)
            for k in (1, 2, 3):
                remote(
                    yr.at[j, k - 1], yr.at[j, k - 1], yss.at[0], yrs.at[j, k - 1], dp, sibling
                ).wait_recv()
                total = total + yr[j, k - 1].astype(F32)
            for half in (0, 1):
                xs[j, half] = total[:, half * 256 : half * 256 + 256].astype(BF16)
                k, copy = x_send(j, half)

                @pl.when(k != 0)
                def _():
                    copy.start()

    def share(k):
        return remote(
            wgp.at[dp], wgp.at[dp], gss.at[k - 1], grs.at[k - 1], (dp + k) % NDP, c
        )

    def x_sum():
        total = xs[xl, xh].astype(F32)
        for k in (1, 2, 3):
            remote(xr.at[k - 1], xr.at[k - 1], xss.at[0], xrs.at[k - 1], dp, sibling).wait_recv()
            total = total + xr[k - 1].astype(F32)
        wgp[dp] = total.astype(BF16)
        for k in range(1, NDP):
            share(k).start()

    def group(g):
        load_q(g).wait()
        load_w(g).wait()
        grad_attn = dot(og2[0], w_v[g], 1, 1).astype(BF16)
        for hh in (0, 1):
            kcols = pl.ds(hh * HEAD, HEAD)
            vcols = pl.ds(GW + hh * HEAD, HEAD)
            keys, values = kvp[g, :, kcols], kvp[g, :, vcols]
            query = q_v[g, :, kcols]
            grad = grad_attn[:, hh * HEAD : (hh + 1) * HEAD]
            scores = dot(keys, query, 1, 1) + bias[...]
            top = jnp.max(scores, axis=0, keepdims=True)
            expo = jnp.exp2((scores - top) * factor)
            probs = expo * (1.0 / jnp.sum(expo, axis=0, keepdims=True))
            low = probs.astype(BF16)
            dprobs = dot(values, grad, 1, 1)
            inner = jnp.sum(probs * dprobs, axis=0, keepdims=True)
            dscores = (probs * (dprobs - inner)).astype(BF16)
            attended = dot(values, low, 0, 0).astype(BF16)

            @pl.when(core == hh)
            def _():
                att_own[g] = attended

            @pl.when(core != hh)
            def _():
                att_out[g] = attended

            grad_q = dot(keys, dscores, 0, 0) * scaling
            dq_st[g, :, kcols] = grad_q.T.astype(BF16)
            grad_k = dot(dscores, query, 1, 0) * scaling
            grad_v = dot(low, grad, 1, 0)
            acc[g, :, kcols] = grad_k[0:TOK]
            acc[g, :, vcols] = grad_v[0:TOK]
            par[g, :, kcols] = grad_k[TOK:736].astype(BF16)
            par[g, :, vcols] = grad_v[TOK:736].astype(BF16)

    pl.semaphore_wait(barrier, len(partners))
    for g in range(GROUPS):
        send_halos(g)
        if g < AHEAD:
            send_level1(g)
        if g == 0:
            load_og.wait()
            og_send.start()
    hop_on(0)

    def step(g, carry):
        for level in range(4):

            @pl.when(takes[level])
            def _():
                fwd(g, level).wait_recv()

            if level == 0:

                @pl.when(hands_on)
                def _():
                    fwd_on(g).start()

        @pl.when(g + AHEAD < GROUPS)
        def _():
            send_level1(g + AHEAD)

        group(g)
        att_send(g).start()
        store_q(g).start()
        send_back(g)

        @pl.when(g + 1 < GROUPS)
        def _():
            hop_on(g + 1)

        @pl.when(g >= 1)
        def _():
            merge_back(g - 1)

            @pl.when(g == 1)
            def _():
                og_send.wait_recv()

            weight_terms(g - 1)

        @pl.when(g >= 3)
        def _():
            hop_back(g - 3)
            z_sum(g - 3)

        return carry

    lax.fori_loop(0, GROUPS, step, 0)
    merge_back(GROUPS - 1)
    weight_terms(GROUPS - 1)

    hop_back(HOPS_B - 1)

    def tail(g, carry):
        @pl.when(g < 3)
        def _():
            z_sum(g + GROUPS - 3)

        @pl.when(g == 4)
        def _():
            y_sum()

        @pl.when(g == 5)
        def _():
            x_sum()

        finish_kv(g)
        return carry

    lax.fori_loop(0, GROUPS, tail, 0)
    for k in range(1, NDP):
        come = wgp.at[(dp - k + NDP) % NDP]
        remote(come, come, gss.at[0], grs.at[k - 1], dp, sibling).wait_recv()
    for part in range(NDP):
        wg_st[:, pl.ds(part * 256, 256)] = wgp[part].astype(F32)
    wg_store = pltpu.make_async_copy(wg_st, wg_hbm, outs.at[GROUPS, 0])
    wg_store.start()

    og_send.wait_send()

    def drain(g, carry):
        store_q(g).wait()
        store_kv(g, 0).wait()
        store_kv(g, 1).wait()
        att_send(g).wait_send()
        for k in (1, 2, 3):
            z_send(g, k).wait_send()

        @pl.when(g % 4 != y)
        def _():
            y_send(g).wait_send()

        for level in range(4):

            @pl.when(sends[level])
            def _():
                fwd(g, level).wait_send()

        @pl.when(hops_f)
        def _():
            fwd_hop(g).wait_send()

        @pl.when(jnp.logical_and(jnp.logical_and(c % 4 == 0, c <= 8), g < HOPS_B))
        def _():
            bwd_hop(g).wait_send()

        @pl.when(hands_on)
        def _():
            fwd_on(g).wait_send()
            bwd(g, 1).wait_send()

        @pl.when(c >= 1)
        def _():
            bwd(g, 0).wait_send()

        @pl.when(jnp.logical_and(odd, c >= 3))
        def _():
            bwd_relay(g).wait_send()

        @pl.when(c >= 4)
        def _():
            bwd(g, 2).wait_send()

        @pl.when(c >= 8)
        def _():
            bwd(g, 3).wait_send()

        return carry

    lax.fori_loop(0, GROUPS, drain, 0)
    for j in (0, 1):
        for half in (0, 1):
            k, copy = x_send(j, half)

            @pl.when(k != 0)
            def _():
                copy.wait_send()

    for k in range(1, NDP):
        share(k).wait_send()
    wg_store.wait()


def move_kernel(*refs):
    ins, outs, bufs, sems = refs[:4], refs[4:8], refs[8:12], refs[12]
    first, second = [], []
    for i in range(4):
        a, b = (ins[i].at[0], outs[i].at[0]) if i < 3 else (ins[i], outs[i])
        n = a.shape[0] // 2
        for j in range(2):
            rows = pl.ds(j * n, n)
            first.append(pltpu.make_async_copy(a.at[rows], bufs[i].at[rows], sems.at[0, i, j]))
            second.append(pltpu.make_async_copy(bufs[i].at[rows], b.at[rows], sems.at[1, i, j]))
    for copy in first:
        copy.start()
    for copy, then in zip(first, second):
        copy.wait()
        then.start()
    for copy in second:
        copy.wait()


def move_out(results):
    return pl.pallas_call(
        move_kernel,
        out_shape=tuple(jax.ShapeDtypeStruct(r.shape, r.dtype) for r in results),
        in_specs=[pl.BlockSpec(memory_space=pl.ANY)] * 4,
        out_specs=(pl.BlockSpec(memory_space=pl.ANY),) * 4,
        scratch_shapes=[pltpu.VMEM(r.shape[-2:], r.dtype) for r in results]
        + [pltpu.SemaphoreType.DMA((2, 4, 2))],
        name="move_out",
    )(*results)


def per_device(query_in, key_in, value_in, out_grad, out_weight):
    vm = pltpu.VMEM
    dma = pltpu.SemaphoreType.DMA
    g = GROUPS
    results = pl.pallas_call(
        kernel,
        out_shape=(
            jax.ShapeDtypeStruct((1, TOK, 2048), BF16),
            jax.ShapeDtypeStruct((1, TOK, 2048), BF16),
            jax.ShapeDtypeStruct((1, TOK, 2048), BF16),
            jax.ShapeDtypeStruct((128, 2048), F32),
        ),
        in_specs=[pl.BlockSpec(memory_space=pl.ANY)] * 5,
        out_specs=(pl.BlockSpec(memory_space=pl.ANY),) * 4,
        scratch_shapes=[
            vm((g, TOK, GW), BF16),
            vm((g, TOK, 2 * GW), BF16),
            vm((2, TOK, 2048), BF16),
            vm((g, GW, 2048), BF16),
            vm((g, KEYS, 2 * GW), BF16),
            vm((g, 480, 2 * GW), BF16),
            vm((g, 128, 2 * GW), BF16),
            vm((g, 480, 2 * GW), BF16),
            vm((g, TOK, 2 * GW), F32),
            vm((g, TOK, 2 * GW), BF16),
            vm((HOPS_B, TOK, 2 * GW), BF16),
            vm((g, HEAD, TOK), BF16),
            vm((g, HEAD, TOK), BF16),
            vm((g, HEAD, TOK), BF16),
            vm((g, 4, HEAD, 512), BF16),
            vm((g, 3, HEAD, 512), BF16),
            vm((g, HEAD, 512), BF16),
            vm((2, 3, HEAD, 512), BF16),
            vm((2, 2, HEAD, 256), BF16),
            vm((3, HEAD, 256), BF16),
            vm((NDP, HEAD, 256), BF16),
            vm((g, TOK, GW), BF16),
            vm((g, TOK, 2 * GW), BF16),
            vm((HEAD, 2048), F32),
            vm((KEYS, TOK), F32),
            vm((TOK, TOK), BF16),
            vm((TOK, TOK), BF16),
            dma((g + 1, 4)),
            dma((g, 5)),
            dma((g, 5)),
            dma((g, 6)),
            dma((g, 6)),
            dma((g,)),
            dma((g,)),
            dma((2,)),
            dma((g, 3)),
            dma((g, 3)),
            dma((g,)),
            dma((2, 3)),
            dma((4,)),
            dma((3,)),
            dma((NDP - 1,)),
            dma((NDP - 1,)),
            dma((g + 1, 3)),
        ],
        compiler_params=pltpu.CompilerParams(
            collective_id=0, has_side_effects=True, vmem_limit_bytes=60 * 2**20
        ),
        name="logsparse_backward",
    )(query_in, key_in, value_in, out_grad, out_weight)
    return move_out(results)


def solution(mesh):
    return jax.shard_map(
        per_device,
        mesh=mesh,
        in_specs=(
            P("dp", "seq", None),
            P("dp", "seq", None),
            P("dp", "seq", None),
            P("dp", "seq", None),
            P(),
        ),
        out_specs=(
            P("dp", "seq", None),
            P("dp", "seq", None),
            P("dp", "seq", None),
            P("seq", None),
        ),
        check_vma=False,
    )
```

```python
import functools
import math

import jax
import jax.numpy as jnp
from jax import lax
from jax.experimental import pallas as pl
from jax.experimental.pallas import tpu as pltpu
from jax.sharding import PartitionSpec as P

HEAD = 128
TOK = 256
GROUPS = 8
GW = 256
KEYS = 768
ROWS = (256, 128, 64, 32)
OFFS = (256, 512, 640, 704)
NSEQ = 16
NDP = 8
AHEAD = 3
LATE = 1
LAG2, LAG3 = 3, 5
HOPS_B = 6
MESH = pl.DeviceIdType.MESH
F32 = jnp.float32
BF16 = jnp.bfloat16


def dot(a, b, ca, cb):
    return lax.dot_general(a, b, (((ca,), (cb,)), ((), ())), preferred_element_type=F32)


def cols_of(g):
    return pl.ds(pl.multiple_of(((g % 4) * 2 + g // 4) * GW, GW), GW)


def row_of(p):
    return jnp.where(
        p < 32,
        8 * p,
        jnp.where(
            p < 64, 8 * (p - 32) + 4, jnp.where(p < 128, 4 * (p - 64) + 2, 2 * (p - 128) + 1)
        ),
    )


def kernel(
    q_hbm, k_hbm, v_hbm, og_hbm, w_hbm,
    dq_hbm, dk_hbm, dv_hbm, wg_hbm,
    q_v, raw, og2, w_v, kvp, par, relay, ret, acc, hop_f, hop_b, att_own, att_out, att_in,
    wa, wb, zr_a, xa, xs_a, xr_a, xr_b, zs_b, zr_b, ys, yr, xm, xs, xr, wgp, dq_st, dkv_st, wg_st, bias, pm, pmt,
    ld, fs, fr, bs, br, ats, atr, ogs, zas, zar, zbs, zbr, xas, xar, yss, yrs, xss, gss, grs, outs,
):
    scaling = 1.0 / math.sqrt(HEAD)
    factor = scaling * math.log2(math.e)
    dp, c = lax.axis_index("dp"), lax.axis_index("seq")
    z, xh = dp // 2, dp % 2
    y, xl, core = c // 4, (c // 2) % 2, c % 2
    even, odd = core == 0, core == 1
    sibling = c + 1 - 2 * core

    def remote(src, dst, ss, rs, to_dp, to_c):
        return pltpu.make_async_remote_copy(
            src_ref=src, dst_ref=dst, send_sem=ss, recv_sem=rs,
            device_id=(to_dp, to_c), device_id_type=MESH,
        )

    def load_kv(g, which):
        src = (k_hbm, v_hbm)[which]
        return pltpu.make_async_copy(
            src.at[0, :, cols_of(g)], raw.at[g, :, pl.ds(which * GW, GW)], ld.at[g, which]
        )

    def load_q(g):
        return pltpu.make_async_copy(q_hbm.at[0, :, cols_of(g)], q_v.at[g], ld.at[g, 2])

    def load_w(g):
        return pltpu.make_async_copy(w_hbm.at[cols_of(g)], w_v.at[g], ld.at[g, 3])

    load_og = pltpu.make_async_copy(og_hbm.at[0], og2.at[0], ld.at[GROUPS, 0])

    partners = (
        [(dp, (c + d) % NSEQ) for d in (1, 15, 2, 14, 3, 13, 4, 8, 12)]
        + [((dp + d) % NDP, c) for d in range(1, NDP)]
        + [(dp + 1 - 2 * xh, c + 2 - 4 * xl)]
    )
    barrier = pltpu.get_barrier_semaphore()
    for partner in partners:
        pl.semaphore_signal(barrier, inc=1, device_id=partner, device_id_type=MESH)
    for g in range(GROUPS):
        load_kv(g, 0).start()
        load_kv(g, 1).start()
        if g == 0:
            load_og.start()
        load_q(g).start()
        load_w(g).start()

    pos0 = lax.broadcasted_iota(jnp.int32, (TOK, TOK), 0)
    pos1 = lax.broadcasted_iota(jnp.int32, (TOK, TOK), 1)
    pm[...] = (row_of(pos0) == pos1).astype(F32).astype(BF16)
    pmt[...] = (row_of(pos1) == pos0).astype(F32).astype(BF16)
    bias[0:TOK] = jnp.where(row_of(pos0) <= pos1, 0.0, -1e30).astype(F32)
    for level in range(4):
        shown = jnp.where(c >= 2**level, 0.0, -1e30).astype(F32)
        bias[pl.ds(OFFS[level], ROWS[level])] = jnp.full((ROWS[level], TOK), shown, F32)

        @pl.when(c < 2**level)
        def _():
            for g in range(GROUPS):
                kvp[g, pl.ds(OFFS[level], ROWS[level])] = jnp.zeros((ROWS[level], 2 * GW), BF16)

    bias[pl.ds(736, 32)] = jnp.full((32, TOK), -1e30, F32)
    for g in range(GROUPS):
        kvp[g, pl.ds(736, 32)] = jnp.zeros((32, 2 * GW), BF16)

    def fwd(g, level):
        return remote(
            kvp.at[g, pl.ds(0, ROWS[level])], kvp.at[g, pl.ds(OFFS[level], ROWS[level])],
            fs.at[g, level], fr.at[g, level], dp, (c + 2**level) % NSEQ,
        )

    def fwd_on(g):
        return remote(
            kvp.at[g, pl.ds(OFFS[0], ROWS[1])], kvp.at[g, pl.ds(OFFS[1], ROWS[1])],
            fs.at[g, 4], fr.at[g, 1], dp, sibling,
        )

    sends = (c < 15, jnp.logical_and(even, c < 14), c < 12, c < 8)
    takes = (c >= 1, c >= 2, c >= 4, c >= 8)
    hands_on = jnp.logical_and(even, c >= 2)

    turns_f = jnp.logical_and(c % 4 == 3, c < 15)
    hops_f = jnp.logical_and(c % 4 == 3, c >= 7)

    def fwd_turn(g):
        return remote(
            kvp.at[g, pl.ds(0, TOK)], hop_f.at[g], fs.at[g, 0], fr.at[g, 4], dp, (c + 4) % NSEQ
        )

    def fwd_hop(g):
        return remote(
            hop_f.at[g], kvp.at[g, pl.ds(OFFS[0], TOK)], fs.at[g, 4], fr.at[g, 0],
            dp, (c - 3 + NSEQ) % NSEQ,
        )

    def hop_on(g):
        @pl.when(hops_f)
        def _():
            fwd_turn(g).wait_recv()
            fwd_hop(g).start()

    def send_level1(g):
        @pl.when(sends[1])
        def _():
            fwd(g, 1).start()

    def send_halos(g):
        load_kv(g, 0).wait()
        load_kv(g, 1).wait()
        kvp[g, pl.ds(0, TOK)] = dot(pm[...], raw[g], 1, 0).astype(BF16)

        @pl.when(turns_f)
        def _():
            fwd_turn(g).start()

        @pl.when(jnp.logical_and(c % 4 != 3, sends[0]))
        def _():
            fwd(g, 0).start()

        for level in (2, 3):

            @pl.when(sends[level])
            def _():
                fwd(g, level).start()

    def bwd(g, level):
        return remote(
            par.at[g, pl.ds(OFFS[level] - TOK, ROWS[level])],
            ret.at[g, pl.ds(OFFS[level] - TOK, ROWS[level])],
            bs.at[g, level], br.at[g, level], dp, (c - 2**level + NSEQ) % NSEQ,
        )

    def bwd_relay(g):
        return remote(
            par.at[g, pl.ds(OFFS[1] - TOK, ROWS[1])], relay.at[g],
            bs.at[g, 1], br.at[g, 4], dp, sibling,
        )

    def turns_b(g):
        return jnp.logical_and(jnp.logical_and(c % 4 == 0, c >= 4), g < HOPS_B)

    def bwd_turn(g):
        return remote(
            par.at[g, pl.ds(0, TOK)], hop_b.at[g], bs.at[g, 0], br.at[g, 5],
            dp, (c - 4 + NSEQ) % NSEQ,
        )

    def bwd_hop(g):
        return remote(
            hop_b.at[g], ret.at[g, pl.ds(0, TOK)], bs.at[g, 5], br.at[g, 0], dp, (c + 3) % NSEQ
        )

    late = c % 4 == 2

    def send_back(g):
        @pl.when(odd)
        def _():
            bwd(g, 0).start()

        @pl.when(jnp.logical_and(odd, c >= 3))
        def _():
            bwd_relay(g).start()

        @pl.when(jnp.logical_and(hands_on, jnp.logical_not(late)))
        def _():
            bwd(g, 1).start()

        @pl.when(c >= 4)
        def _():
            bwd(g, 2).start()

        @pl.when(c >= 8)
        def _():
            bwd(g, 3).start()

    def merge_back(g):
        @pl.when(hands_on)
        def _():
            bwd_relay(g).wait_recv()
            merged = par[g, pl.ds(0, ROWS[1])].astype(F32) + relay[g].astype(F32)
            par[g, pl.ds(0, ROWS[1])] = merged.astype(BF16)

            @pl.when(turns_b(g))
            def _():
                bwd_turn(g).start()

            @pl.when(jnp.logical_not(turns_b(g)))
            def _():
                bwd(g, 0).start()

    def late_back(g):
        bwd(g, 1).start()
        merge_back(g)

    def hop_back(g):
        @pl.when(jnp.logical_and(c % 4 == 0, c <= 8))
        def _():
            bwd_turn(g).wait_recv()
            bwd_hop(g).start()

    comes_back = (c < 15, jnp.logical_and(even, c < 14), c < 12, c < 8)

    def store_kv(g, which):
        dst = (dk_hbm, dv_hbm)[which]
        return pltpu.make_async_copy(
            dkv_st.at[g, :, pl.ds(which * GW, GW)],
            dst.at[0, :, cols_of(g)],
            outs.at[g, which],
        )

    def store_q(g):
        return pltpu.make_async_copy(
            dq_st.at[g], dq_hbm.at[0, :, cols_of(g)], outs.at[g, 2]
        )

    def finish_kv(g):
        for level in range(4):

            @pl.when(comes_back[level])
            def _():
                bwd(g, level).wait_recv()
                acc[g, pl.ds(0, ROWS[level])] += ret[
                    g, pl.ds(OFFS[level] - TOK, ROWS[level])
                ].astype(F32)

        dkv_st[g] = dot(pmt[...], acc[g].astype(BF16), 1, 0).astype(BF16)
        store_kv(g, 0).start()
        store_kv(g, 1).start()

    def att_send(g):
        return remote(att_out.at[g], att_in.at[g], ats.at[g], atr.at[g], dp, sibling)

    og_send = remote(og2.at[0], og2.at[1], ogs.at[0], ogs.at[1], dp, sibling)

    def z_send_a(g, k):
        to = (z + k) % 4
        return remote(
            wa.at[g, to], zr_a.at[g, k - 1], zas.at[g, k - 1], zar.at[g, k - 1], to * 2 + xh, c
        )

    def z_send_b(g, k):
        to = (z + k) % 4
        return remote(
            zs_b.at[g, to], zr_b.at[g, k - 1], zbs.at[g, k - 1], zbr.at[g, k - 1], to * 2 + xh, c
        )

    across = (dp + 1 - 2 * xh, c + 2 - 4 * xl)

    def x_send_a(g):
        return remote(xs_a.at[g], xr_a.at[g], xas.at[g, 0], xar.at[g, 0], *across)

    def x_send_b(g):
        return remote(wb.at[g, 1 - xh], xr_b.at[g], xas.at[g, 1], xar.at[g, 1], *across)

    def weight_terms(g):
        att_send(g).wait_recv()
        for part in range(4):
            cols = pl.ds(part * 512, 512)
            terms = dot(att_own[g], og2[0, :, cols], 1, 0) + dot(att_in[g], og2[1, :, cols], 1, 0)
            terms = terms.astype(BF16)
            if part < 2:
                wa[g, 2 * part] = terms[:, 0:256]
                wa[g, 2 * part + 1] = terms[:, 256:512]
            else:
                for q in range(4):
                    wb[g, q % 2, 2 * (part - 2) + q // 2] = terms[:, q * 128 : q * 128 + 128]
        for k in (1, 2, 3):
            z_send_a(g, k).start()
        x_send_b(g).start()

    def second_sums(g):
        for k in (1, 2, 3):
            z_send_a(g, k).wait_recv()
        total = wa[g, z].astype(F32)
        for k in (1, 2, 3):
            total = total + zr_a[g, k - 1].astype(F32)
        left, right = total[:, 0:128], total[:, 128:256]
        xa[g] = jnp.where(xh == 0, left, right)
        xs_a[g] = jnp.where(xh == 0, right, left).astype(BF16)
        x_send_a(g).start()
        x_send_b(g).wait_recv()
        for part in range(4):
            zs_b[g, part] = (wb[g, xh, part].astype(F32) + xr_b[g, part].astype(F32)).astype(BF16)
        for k in (1, 2, 3):
            z_send_b(g, k).start()

    def y_send(g):
        k = (g % 4 - y + 4) % 4
        return remote(
            ys.at[g], yr.at[g // 4, k - 1], yss.at[g], yrs.at[g // 4, k - 1],
            dp, (g % 4) * 4 + c % 4,
        )

    def third_sums(g):
        x_send_a(g).wait_recv()
        for k in (1, 2, 3):
            z_send_b(g, k).wait_recv()
        ys[g, :, 0:128] = (xa[g] + xr_a[g].astype(F32)).astype(BF16)
        total = zs_b[g, z].astype(F32)
        for k in (1, 2, 3):
            total = total + zr_b[g, k - 1].astype(F32)
        ys[g, :, 128:256] = total.astype(BF16)

        @pl.when(g % 4 != y)
        def _():
            y_send(g).start()

    x_send = remote(xs, xr, xss.at[0], xss.at[1], dp, c + 2 - 4 * xl)

    def y_sum():
        totals = []
        for j in (0, 1):
            total = ys[y + 4 * j].astype(F32)
            for k in (1, 2, 3):
                remote(
                    yr.at[j, k - 1], yr.at[j, k - 1], yss.at[0], yrs.at[j, k - 1], dp, sibling
                ).wait_recv()
                total = total + yr[j, k - 1].astype(F32)
            totals.append(total)
        xm[...] = jnp.where(xl == 0, totals[0], totals[1])
        xs[...] = jnp.where(xl == 0, totals[1], totals[0]).astype(BF16)
        x_send.start()

    def share(k):
        return remote(
            wgp.at[dp], wgp.at[dp], gss.at[k - 1], grs.at[k - 1], (dp + k) % NDP, c
        )

    def x_sum():
        x_send.wait_recv()
        wgp[dp] = (xm[...] + xr[...].astype(F32)).astype(BF16)
        for k in range(1, NDP):
            share(k).start()

    def group(g):
        load_q(g).wait()
        load_w(g).wait()
        grad_attn = dot(og2[0], w_v[g], 1, 1).astype(BF16)
        for hh in (0, 1):
            kcols = pl.ds(hh * HEAD, HEAD)
            vcols = pl.ds(GW + hh * HEAD, HEAD)
            keys, values = kvp[g, :, kcols], kvp[g, :, vcols]
            query = q_v[g, :, kcols]
            grad = grad_attn[:, hh * HEAD : (hh + 1) * HEAD]
            scores = dot(keys, query, 1, 1) + bias[...]
            top = jnp.max(scores, axis=0, keepdims=True)
            expo = jnp.exp2((scores - top) * factor)
            probs = expo * (1.0 / jnp.sum(expo, axis=0, keepdims=True))
            low = probs.astype(BF16)
            dprobs = dot(values, grad, 1, 1)
            inner = jnp.sum(probs * dprobs, axis=0, keepdims=True)
            dscores = (probs * (dprobs - inner)).astype(BF16)
            attended = dot(values, low, 0, 0).astype(BF16)

            @pl.when(core == hh)
            def _():
                att_own[g] = attended

            @pl.when(core != hh)
            def _():
                att_out[g] = attended

            grad_q = dot(keys, dscores, 0, 0) * scaling
            dq_st[g, :, kcols] = grad_q.T.astype(BF16)
            grad_k = dot(dscores, query, 1, 0) * scaling
            grad_v = dot(low, grad, 1, 0)
            acc[g, :, kcols] = grad_k[0:TOK]
            acc[g, :, vcols] = grad_v[0:TOK]
            par[g, :, kcols] = grad_k[TOK:736].astype(BF16)
            par[g, :, vcols] = grad_v[TOK:736].astype(BF16)

    pl.semaphore_wait(barrier, len(partners))
    for g in range(GROUPS):
        send_halos(g)
        if g < AHEAD:
            send_level1(g)
        if g == 0:
            load_og.wait()
            og_send.start()
    hop_on(0)

    def step(g, carry):
        for level in range(4):

            @pl.when(takes[level])
            def _():
                fwd(g, level).wait_recv()

            if level == 0:

                @pl.when(hands_on)
                def _():
                    fwd_on(g).start()

        @pl.when(g + AHEAD < GROUPS)
        def _():
            send_level1(g + AHEAD)

        group(g)
        att_send(g).start()
        store_q(g).start()
        send_back(g)

        @pl.when(g + 1 < GROUPS)
        def _():
            hop_on(g + 1)

        @pl.when(jnp.logical_and(g >= 1, jnp.logical_not(late)))
        def _():
            merge_back(g - 1)

        @pl.when(jnp.logical_and(g >= LATE, late))
        def _():
            late_back(g - LATE)

        @pl.when(g == 1)
        def _():
            og_send.wait_recv()

        @pl.when(g >= 1)
        def _():
            weight_terms(g - 1)

        @pl.when(g >= 3)
        def _():
            hop_back(g - 3)

        @pl.when(g >= LAG2)
        def _():
            second_sums(g - LAG2)

        @pl.when(g >= LAG3)
        def _():
            third_sums(g - LAG3)

        return carry

    lax.fori_loop(0, GROUPS, step, 0)

    @pl.when(jnp.logical_not(late))
    def _():
        merge_back(GROUPS - 1)

    weight_terms(GROUPS - 1)

    @pl.when(late)
    def _():
        lax.fori_loop(GROUPS - LATE, GROUPS, lambda g, carry: late_back(g) or carry, 0)

    hop_back(HOPS_B - 1)

    def tail(i, carry):
        @pl.when(jnp.logical_and(i >= GROUPS, i < GROUPS + LAG2))
        def _():
            second_sums(i - LAG2)

        @pl.when(i < GROUPS + LAG3)
        def _():
            third_sums(i - LAG3)

        return carry

    lax.fori_loop(GROUPS, GROUPS + LAG3, tail, 0)

    def last(g, carry):
        finish_kv(g)

        @pl.when(g == 1)
        def _():
            y_sum()

        @pl.when(g == 3)
        def _():
            x_sum()

        return carry

    lax.fori_loop(0, GROUPS, last, 0)
    for k in range(1, NDP):
        come = wgp.at[(dp - k + NDP) % NDP]
        remote(come, come, gss.at[0], grs.at[k - 1], dp, sibling).wait_recv()
    for part in range(NDP):
        wg_st[:, pl.ds(part * 128, 128)] = wgp[part, :, 0:128].astype(F32)
        wg_st[:, pl.ds(1024 + part * 128, 128)] = wgp[part, :, 128:256].astype(F32)
    wg_store = pltpu.make_async_copy(wg_st, wg_hbm, outs.at[GROUPS, 0])
    wg_store.start()

    og_send.wait_send()

    def drain(g, carry):
        store_q(g).wait()
        store_kv(g, 0).wait()
        store_kv(g, 1).wait()
        att_send(g).wait_send()
        for k in (1, 2, 3):
            z_send_a(g, k).wait_send()
            z_send_b(g, k).wait_send()
        x_send_a(g).wait_send()
        x_send_b(g).wait_send()

        @pl.when(g % 4 != y)
        def _():
            y_send(g).wait_send()

        for level in range(4):

            @pl.when(sends[level])
            def _():
                fwd(g, level).wait_send()

        @pl.when(hops_f)
        def _():
            fwd_hop(g).wait_send()

        @pl.when(jnp.logical_and(jnp.logical_and(c % 4 == 0, c <= 8), g < HOPS_B))
        def _():
            bwd_hop(g).wait_send()

        @pl.when(hands_on)
        def _():
            fwd_on(g).wait_send()
            bwd(g, 1).wait_send()

        @pl.when(c >= 1)
        def _():
            bwd(g, 0).wait_send()

        @pl.when(jnp.logical_and(odd, c >= 3))
        def _():
            bwd_relay(g).wait_send()

        @pl.when(c >= 4)
        def _():
            bwd(g, 2).wait_send()

        @pl.when(c >= 8)
        def _():
            bwd(g, 3).wait_send()

        return carry

    lax.fori_loop(0, GROUPS, drain, 0)
    x_send.wait_send()
    for k in range(1, NDP):
        share(k).wait_send()
    wg_store.wait()


def move_kernel(*refs):
    ins, outs, bufs, sems = refs[:4], refs[4:8], refs[8:12], refs[12]
    first, second = [], []
    for i in range(4):
        a, b = (ins[i].at[0], outs[i].at[0]) if i < 3 else (ins[i], outs[i])
        n = a.shape[0] // 2
        for j in range(2):
            rows = pl.ds(j * n, n)
            first.append(pltpu.make_async_copy(a.at[rows], bufs[i].at[rows], sems.at[0, i, j]))
            second.append(pltpu.make_async_copy(bufs[i].at[rows], b.at[rows], sems.at[1, i, j]))
    for copy in first:
        copy.start()
    for copy, then in zip(first, second):
        copy.wait()
        then.start()
    for copy in second:
        copy.wait()


def move_out(results):
    return pl.pallas_call(
        move_kernel,
        out_shape=tuple(jax.ShapeDtypeStruct(r.shape, r.dtype) for r in results),
        in_specs=[pl.BlockSpec(memory_space=pl.ANY)] * 4,
        out_specs=(pl.BlockSpec(memory_space=pl.ANY),) * 4,
        scratch_shapes=[pltpu.VMEM(r.shape[-2:], r.dtype) for r in results]
        + [pltpu.SemaphoreType.DMA((2, 4, 2))],
        name="move_out",
    )(*results)


def per_device(query_in, key_in, value_in, out_grad, out_weight):
    vm = pltpu.VMEM
    dma = pltpu.SemaphoreType.DMA
    g = GROUPS
    results = pl.pallas_call(
        kernel,
        out_shape=(
            jax.ShapeDtypeStruct((1, TOK, 2048), BF16),
            jax.ShapeDtypeStruct((1, TOK, 2048), BF16),
            jax.ShapeDtypeStruct((1, TOK, 2048), BF16),
            jax.ShapeDtypeStruct((128, 2048), F32),
        ),
        in_specs=[pl.BlockSpec(memory_space=pl.ANY)] * 5,
        out_specs=(pl.BlockSpec(memory_space=pl.ANY),) * 4,
        scratch_shapes=[
            vm((g, TOK, GW), BF16),
            vm((g, TOK, 2 * GW), BF16),
            vm((2, TOK, 2048), BF16),
            vm((g, GW, 2048), BF16),
            vm((g, KEYS, 2 * GW), BF16),
            vm((g, 480, 2 * GW), BF16),
            vm((g, 128, 2 * GW), BF16),
            vm((g, 480, 2 * GW), BF16),
            vm((g, TOK, 2 * GW), F32),
            vm((g, TOK, 2 * GW), BF16),
            vm((HOPS_B, TOK, 2 * GW), BF16),
            vm((g, HEAD, TOK), BF16),
            vm((g, HEAD, TOK), BF16),
            vm((g, HEAD, TOK), BF16),
            vm((g, 4, HEAD, 256), BF16),
            vm((g, 2, 4, HEAD, 128), BF16),
            vm((g, 3, HEAD, 256), BF16),
            vm((g, HEAD, 128), F32),
            vm((g, HEAD, 128), BF16),
            vm((g, HEAD, 128), BF16),
            vm((g, 4, HEAD, 128), BF16),
            vm((g, 4, HEAD, 128), BF16),
            vm((g, 3, HEAD, 128), BF16),
            vm((g, HEAD, 256), BF16),
            vm((2, 3, HEAD, 256), BF16),
            vm((HEAD, 256), F32),
            vm((HEAD, 256), BF16),
            vm((HEAD, 256), BF16),
            vm((NDP, HEAD, 256), BF16),
            vm((g, TOK, GW), BF16),
            vm((g, TOK, 2 * GW), BF16),
            vm((HEAD, 2048), F32),
            vm((KEYS, TOK), F32),
            vm((TOK, TOK), BF16),
            vm((TOK, TOK), BF16),
            dma((g + 1, 4)),
            dma((g, 5)),
            dma((g, 5)),
            dma((g, 6)),
            dma((g, 6)),
            dma((g,)),
            dma((g,)),
            dma((2,)),
            dma((g, 3)),
            dma((g, 3)),
            dma((g, 3)),
            dma((g, 3)),
            dma((g, 2)),
            dma((g, 2)),
            dma((g,)),
            dma((2, 3)),
            dma((2,)),
            dma((NDP - 1,)),
            dma((NDP - 1,)),
            dma((g + 1, 3)),
        ],
        compiler_params=pltpu.CompilerParams(
            collective_id=0, has_side_effects=True, vmem_limit_bytes=60 * 2**20
        ),
        name="logsparse_backward",
    )(query_in, key_in, value_in, out_grad, out_weight)
    return move_out(results)


def solution(mesh):
    return jax.shard_map(
        per_device,
        mesh=mesh,
        in_specs=(
            P("dp", "seq", None),
            P("dp", "seq", None),
            P("dp", "seq", None),
            P("dp", "seq", None),
            P(),
        ),
        out_specs=(
            P("dp", "seq", None),
            P("dp", "seq", None),
            P("dp", "seq", None),
            P("seq", None),
        ),
        check_vma=False,
    )
```

```python
import functools
import math

import jax
import jax.numpy as jnp
from jax import lax
from jax.experimental import pallas as pl
from jax.experimental.pallas import tpu as pltpu
from jax.sharding import PartitionSpec as P

HEAD = 128
TOK = 256
GROUPS = 8
GW = 256
KEYS = 768
ROWS = (256, 128, 64, 32)
OFFS = (256, 512, 640, 704)
NSEQ = 16
NDP = 8
AHEAD = 3
LATE = 1
LAG2, LAG3 = 3, 5
HOPS_B = 6
MESH = pl.DeviceIdType.MESH
F32 = jnp.float32
BF16 = jnp.bfloat16


def dot(a, b, ca, cb):
    return lax.dot_general(a, b, (((ca,), (cb,)), ((), ())), preferred_element_type=F32)


def cols_of(g):
    return pl.ds(pl.multiple_of(((g % 4) * 2 + g // 4) * GW, GW), GW)


def row_of(p):
    return jnp.where(
        p < 32,
        8 * p,
        jnp.where(
            p < 64, 8 * (p - 32) + 4, jnp.where(p < 128, 4 * (p - 64) + 2, 2 * (p - 128) + 1)
        ),
    )


def kernel(
    q_hbm, k_hbm, v_hbm, og_hbm, w_hbm,
    dq_hbm, dk_hbm, dv_hbm, wg_hbm,
    q_v, raw, og2, w_v, kvp, par, relay, ret, acc, hop_f, hop_b, att_own, att_out, att_in,
    wa, wb, zr_a, xa, xs_a, xr_a, xr_b, zs_b, zr_b, ys, yr, xm, xs, xr, wgp, dq_st, dkv_st, wg_st, bias, pm, pmt,
    ld, fs, fr, bs, br, ats, atr, ogs, zas, zar, zbs, zbr, xas, xar, yss, yrs, xss, gss, grs, outs,
):
    scaling = 1.0 / math.sqrt(HEAD)
    factor = scaling * math.log2(math.e)
    dp, c = lax.axis_index("dp"), lax.axis_index("seq")
    z, xh = dp // 2, dp % 2
    y, xl, core = c // 4, (c // 2) % 2, c % 2
    even, odd = core == 0, core == 1
    sibling = c + 1 - 2 * core

    def remote(src, dst, ss, rs, to_dp, to_c):
        return pltpu.make_async_remote_copy(
            src_ref=src, dst_ref=dst, send_sem=ss, recv_sem=rs,
            device_id=(to_dp, to_c), device_id_type=MESH,
        )

    def load_kv(g, which):
        src = (k_hbm, v_hbm)[which]
        return pltpu.make_async_copy(
            src.at[0, :, cols_of(g)], raw.at[g, :, pl.ds(which * GW, GW)], ld.at[g, which]
        )

    def load_q(g):
        return pltpu.make_async_copy(q_hbm.at[0, :, cols_of(g)], q_v.at[g], ld.at[g, 2])

    def load_w(g):
        return pltpu.make_async_copy(w_hbm.at[cols_of(g)], w_v.at[g], ld.at[g, 3])

    load_og = pltpu.make_async_copy(og_hbm.at[0], og2.at[0], ld.at[GROUPS, 0])

    partners = (
        [(dp, (c + d) % NSEQ) for d in (1, 15, 2, 14, 3, 13, 4, 8, 12)]
        + [((dp + d) % NDP, c) for d in range(1, NDP)]
        + [(dp + 1 - 2 * xh, c + 2 - 4 * xl)]
    )
    barrier = pltpu.get_barrier_semaphore()
    for partner in partners:
        pl.semaphore_signal(barrier, inc=1, device_id=partner, device_id_type=MESH)
    for g in range(GROUPS):
        load_kv(g, 0).start()
        load_kv(g, 1).start()
        if g == 0:
            load_og.start()
        load_q(g).start()
        load_w(g).start()

    pos0 = lax.broadcasted_iota(jnp.int32, (TOK, TOK), 0)
    pos1 = lax.broadcasted_iota(jnp.int32, (TOK, TOK), 1)
    pm[...] = (row_of(pos0) == pos1).astype(F32).astype(BF16)
    pmt[...] = (row_of(pos1) == pos0).astype(F32).astype(BF16)
    bias[0:TOK] = jnp.where(row_of(pos0) <= pos1, 0.0, -1e30).astype(F32)
    for level in range(4):
        shown = jnp.where(c >= 2**level, 0.0, -1e30).astype(F32)
        bias[pl.ds(OFFS[level], ROWS[level])] = jnp.full((ROWS[level], TOK), shown, F32)

        @pl.when(c < 2**level)
        def _():
            for g in range(GROUPS):
                kvp[g, pl.ds(OFFS[level], ROWS[level])] = jnp.zeros((ROWS[level], 2 * GW), BF16)

    bias[pl.ds(736, 32)] = jnp.full((32, TOK), -1e30, F32)
    for g in range(GROUPS):
        kvp[g, pl.ds(736, 32)] = jnp.zeros((32, 2 * GW), BF16)

    def fwd(g, level):
        return remote(
            kvp.at[g, pl.ds(0, ROWS[level])], kvp.at[g, pl.ds(OFFS[level], ROWS[level])],
            fs.at[g, level], fr.at[g, level], dp, (c + 2**level) % NSEQ,
        )

    def fwd_on(g):
        return remote(
            kvp.at[g, pl.ds(OFFS[0], ROWS[1])], kvp.at[g, pl.ds(OFFS[1], ROWS[1])],
            fs.at[g, 4], fr.at[g, 1], dp, sibling,
        )

    sends = (c < 15, jnp.logical_and(even, c < 14), c < 12, c < 8)
    takes = (c >= 1, c >= 2, c >= 4, c >= 8)
    hands_on = jnp.logical_and(even, c >= 2)

    turns_f = jnp.logical_and(c % 4 == 3, c < 15)
    hops_f = jnp.logical_and(c % 4 == 3, c >= 7)

    def fwd_turn(g):
        return remote(
            kvp.at[g, pl.ds(0, TOK)], hop_f.at[g], fs.at[g, 0], fr.at[g, 4], dp, (c + 4) % NSEQ
        )

    def fwd_hop(g):
        return remote(
            hop_f.at[g], kvp.at[g, pl.ds(OFFS[0], TOK)], fs.at[g, 4], fr.at[g, 0],
            dp, (c - 3 + NSEQ) % NSEQ,
        )

    def hop_on(g):
        @pl.when(hops_f)
        def _():
            fwd_turn(g).wait_recv()
            fwd_hop(g).start()

    def send_level1(g):
        @pl.when(sends[1])
        def _():
            fwd(g, 1).start()

    def send_halos(g):
        load_kv(g, 0).wait()
        load_kv(g, 1).wait()
        kvp[g, pl.ds(0, TOK)] = dot(pm[...], raw[g], 1, 0).astype(BF16)

        @pl.when(turns_f)
        def _():
            fwd_turn(g).start()

        @pl.when(jnp.logical_and(c % 4 != 3, sends[0]))
        def _():
            fwd(g, 0).start()

        for level in (2, 3):

            @pl.when(sends[level])
            def _():
                fwd(g, level).start()

    def bwd(g, level):
        return remote(
            par.at[g, pl.ds(OFFS[level] - TOK, ROWS[level])],
            ret.at[g, pl.ds(OFFS[level] - TOK, ROWS[level])],
            bs.at[g, level], br.at[g, level], dp, (c - 2**level + NSEQ) % NSEQ,
        )

    def bwd_relay(g):
        return remote(
            par.at[g, pl.ds(OFFS[1] - TOK, ROWS[1])], relay.at[g],
            bs.at[g, 1], br.at[g, 4], dp, sibling,
        )

    def turns_b(g):
        return jnp.logical_and(jnp.logical_and(c % 4 == 0, c >= 4), g < HOPS_B)

    def bwd_turn(g):
        return remote(
            par.at[g, pl.ds(0, TOK)], hop_b.at[g], bs.at[g, 0], br.at[g, 5],
            dp, (c - 4 + NSEQ) % NSEQ,
        )

    def bwd_hop(g):
        return remote(
            hop_b.at[g], ret.at[g, pl.ds(0, TOK)], bs.at[g, 5], br.at[g, 0], dp, (c + 3) % NSEQ
        )

    late = c % 4 == 2

    def send_back(g):
        @pl.when(odd)
        def _():
            bwd(g, 0).start()

        @pl.when(jnp.logical_and(odd, c >= 3))
        def _():
            bwd_relay(g).start()

        @pl.when(jnp.logical_and(hands_on, jnp.logical_not(late)))
        def _():
            bwd(g, 1).start()

        @pl.when(c >= 4)
        def _():
            bwd(g, 2).start()

        @pl.when(c >= 8)
        def _():
            bwd(g, 3).start()

    def merge_back(g):
        @pl.when(hands_on)
        def _():
            bwd_relay(g).wait_recv()
            merged = par[g, pl.ds(0, ROWS[1])].astype(F32) + relay[g].astype(F32)
            par[g, pl.ds(0, ROWS[1])] = merged.astype(BF16)

            @pl.when(turns_b(g))
            def _():
                bwd_turn(g).start()

            @pl.when(jnp.logical_not(turns_b(g)))
            def _():
                bwd(g, 0).start()

    def late_back(g):
        bwd(g, 1).start()
        merge_back(g)

    def hop_back(g):
        @pl.when(jnp.logical_and(c % 4 == 0, c <= 8))
        def _():
            bwd_turn(g).wait_recv()
            bwd_hop(g).start()

    comes_back = (c < 15, jnp.logical_and(even, c < 14), c < 12, c < 8)

    def store_kv(g, which):
        dst = (dk_hbm, dv_hbm)[which]
        return pltpu.make_async_copy(
            dkv_st.at[g, :, pl.ds(which * GW, GW)],
            dst.at[0, :, cols_of(g)],
            outs.at[g, which],
        )

    def store_q(g):
        return pltpu.make_async_copy(
            dq_st.at[g], dq_hbm.at[0, :, cols_of(g)], outs.at[g, 2]
        )

    def finish_kv(g):
        for level in range(4):

            @pl.when(comes_back[level])
            def _():
                bwd(g, level).wait_recv()
                acc[g, pl.ds(0, ROWS[level])] += ret[
                    g, pl.ds(OFFS[level] - TOK, ROWS[level])
                ].astype(F32)

        dkv_st[g] = dot(pmt[...], acc[g].astype(BF16), 1, 0).astype(BF16)
        store_kv(g, 0).start()
        store_kv(g, 1).start()

    def att_send(g):
        return remote(att_out.at[g], att_in.at[g], ats.at[g], atr.at[g], dp, sibling)

    og_send = remote(og2.at[0], og2.at[1], ogs.at[0], ogs.at[1], dp, sibling)

    def z_send_a(g, k):
        to = (z + k) % 4
        return remote(
            wa.at[g, to], zr_a.at[g, k - 1], zas.at[g, k - 1], zar.at[g, k - 1], to * 2 + xh, c
        )

    def z_send_b(g, k):
        to = (z + k) % 4
        return remote(
            zs_b.at[g, to], zr_b.at[g, k - 1], zbs.at[g, k - 1], zbr.at[g, k - 1], to * 2 + xh, c
        )

    across = (dp + 1 - 2 * xh, c + 2 - 4 * xl)

    def x_send_a(g):
        return remote(xs_a.at[g], xr_a.at[g], xas.at[g, 0], xar.at[g, 0], *across)

    def x_send_b(g):
        return remote(wb.at[g, 1 - xh], xr_b.at[g], xas.at[g, 1], xar.at[g, 1], *across)

    def weight_terms(g):
        att_send(g).wait_recv()
        for part in range(4):
            cols = pl.ds(part * 512, 512)
            terms = dot(att_own[g], og2[0, :, cols], 1, 0) + dot(att_in[g], og2[1, :, cols], 1, 0)
            terms = terms.astype(BF16)
            if part < 2:
                wa[g, 2 * part] = terms[:, 0:256]
                wa[g, 2 * part + 1] = terms[:, 256:512]
            else:
                for q in range(4):
                    wb[g, q % 2, 2 * (part - 2) + q // 2] = terms[:, q * 128 : q * 128 + 128]
        for k in (1, 2, 3):
            z_send_a(g, k).start()
        x_send_b(g).start()

    def second_sums(g):
        for k in (1, 2, 3):
            z_send_a(g, k).wait_recv()
        total = wa[g, z].astype(F32)
        for k in (1, 2, 3):
            total = total + zr_a[g, k - 1].astype(F32)
        left, right = total[:, 0:128], total[:, 128:256]
        xa[g] = jnp.where(xh == 0, left, right)
        xs_a[g] = jnp.where(xh == 0, right, left).astype(BF16)
        x_send_a(g).start()
        x_send_b(g).wait_recv()
        for part in range(4):
            zs_b[g, part] = (wb[g, xh, part].astype(F32) + xr_b[g, part].astype(F32)).astype(BF16)
        for k in (1, 2, 3):
            z_send_b(g, k).start()

    def y_send(g):
        k = (g % 4 - y + 4) % 4
        return remote(
            ys.at[g], yr.at[g // 4, k - 1], yss.at[g], yrs.at[g // 4, k - 1],
            dp, (g % 4) * 4 + c % 4,
        )

    def third_sums(g):
        x_send_a(g).wait_recv()
        for k in (1, 2, 3):
            z_send_b(g, k).wait_recv()
        ys[g, :, 0:128] = (xa[g] + xr_a[g].astype(F32)).astype(BF16)
        total = zs_b[g, z].astype(F32)
        for k in (1, 2, 3):
            total = total + zr_b[g, k - 1].astype(F32)
        ys[g, :, 128:256] = total.astype(BF16)

        @pl.when(g % 4 != y)
        def _():
            y_send(g).start()

    x_send = remote(xs, xr, xss.at[0], xss.at[1], dp, c + 2 - 4 * xl)

    def y_sum():
        totals = []
        for j in (0, 1):
            total = ys[y + 4 * j].astype(F32)
            for k in (1, 2, 3):
                remote(
                    yr.at[j, k - 1], yr.at[j, k - 1], yss.at[0], yrs.at[j, k - 1], dp, sibling
                ).wait_recv()
                total = total + yr[j, k - 1].astype(F32)
            totals.append(total)
        xm[...] = jnp.where(xl == 0, totals[0], totals[1])
        xs[...] = jnp.where(xl == 0, totals[1], totals[0]).astype(BF16)
        x_send.start()

    def share(k):
        return remote(
            wgp.at[dp], wgp.at[dp], gss.at[k - 1], grs.at[k - 1], (dp + k) % NDP, c
        )

    def x_sum():
        x_send.wait_recv()
        wgp[dp] = (xm[...] + xr[...].astype(F32)).astype(BF16)
        for k in range(1, NDP):
            share(k).start()

    def group(g):
        load_q(g).wait()
        load_w(g).wait()
        grad_attn = dot(og2[0], w_v[g], 1, 1).astype(BF16)
        for hh in (0, 1):
            kcols = pl.ds(hh * HEAD, HEAD)
            vcols = pl.ds(GW + hh * HEAD, HEAD)
            keys, values = kvp[g, :, kcols], kvp[g, :, vcols]
            query = q_v[g, :, kcols]
            grad = grad_attn[:, hh * HEAD : (hh + 1) * HEAD]
            scores = dot(keys, query, 1, 1) + bias[...]
            top = jnp.max(scores, axis=0, keepdims=True)
            expo = jnp.exp2((scores - top) * factor)
            probs = expo * (1.0 / jnp.sum(expo, axis=0, keepdims=True))
            low = probs.astype(BF16)
            dprobs = dot(values, grad, 1, 1)
            inner = jnp.sum(probs * dprobs, axis=0, keepdims=True)
            dscores = (probs * (dprobs - inner)).astype(BF16)
            attended = dot(values, low, 0, 0).astype(BF16)

            @pl.when(core == hh)
            def _():
                att_own[g] = attended

            @pl.when(core != hh)
            def _():
                att_out[g] = attended

            grad_q = dot(keys, dscores, 0, 0) * scaling
            dq_st[g, :, kcols] = grad_q.T.astype(BF16)
            grad_k = dot(dscores, query, 1, 0) * scaling
            grad_v = dot(low, grad, 1, 0)
            acc[g, :, kcols] = grad_k[0:TOK]
            acc[g, :, vcols] = grad_v[0:TOK]
            par[g, :, kcols] = grad_k[TOK:736].astype(BF16)
            par[g, :, vcols] = grad_v[TOK:736].astype(BF16)

    pl.semaphore_wait(barrier, len(partners))
    for g in range(GROUPS):
        send_halos(g)
        if g < AHEAD:
            send_level1(g)
        if g == 0:
            load_og.wait()
            og_send.start()
    hop_on(0)

    def step(g, carry):
        for level in range(4):

            @pl.when(takes[level])
            def _():
                fwd(g, level).wait_recv()

            if level == 0:

                @pl.when(hands_on)
                def _():
                    fwd_on(g).start()

        @pl.when(g + AHEAD < GROUPS)
        def _():
            send_level1(g + AHEAD)

        group(g)
        att_send(g).start()
        store_q(g).start()
        send_back(g)

        @pl.when(g + 1 < GROUPS)
        def _():
            hop_on(g + 1)

        @pl.when(jnp.logical_and(g >= 1, jnp.logical_not(late)))
        def _():
            merge_back(g - 1)

        @pl.when(jnp.logical_and(g >= LATE, late))
        def _():
            late_back(g - LATE)

        @pl.when(g == 1)
        def _():
            og_send.wait_recv()

        @pl.when(g >= 1)
        def _():
            weight_terms(g - 1)

        @pl.when(g >= 3)
        def _():
            hop_back(g - 3)

        @pl.when(g >= LAG2)
        def _():
            second_sums(g - LAG2)

        @pl.when(g >= LAG3)
        def _():
            third_sums(g - LAG3)

        return carry

    lax.fori_loop(0, GROUPS, step, 0)

    @pl.when(jnp.logical_not(late))
    def _():
        merge_back(GROUPS - 1)

    weight_terms(GROUPS - 1)

    @pl.when(late)
    def _():
        lax.fori_loop(GROUPS - LATE, GROUPS, lambda g, carry: late_back(g) or carry, 0)

    hop_back(HOPS_B - 1)

    def tail(i, carry):
        @pl.when(jnp.logical_and(i >= GROUPS, i < GROUPS + LAG2))
        def _():
            second_sums(i - LAG2)

        @pl.when(i < GROUPS + LAG3)
        def _():
            third_sums(i - LAG3)

        return carry

    lax.fori_loop(GROUPS, GROUPS + LAG3, tail, 0)

    def last(g, carry):
        finish_kv(g)

        @pl.when(g == 1)
        def _():
            y_sum()

        @pl.when(g == 3)
        def _():
            x_sum()

        return carry

    lax.fori_loop(0, GROUPS, last, 0)
    for k in range(1, NDP):
        come = wgp.at[(dp - k + NDP) % NDP]
        remote(come, come, gss.at[0], grs.at[k - 1], dp, sibling).wait_recv()
    for part in range(NDP):
        wg_st[:, pl.ds(part * 128, 128)] = wgp[part, :, 0:128]
        wg_st[:, pl.ds(1024 + part * 128, 128)] = wgp[part, :, 128:256]
    wg_store = pltpu.make_async_copy(wg_st, wg_hbm, outs.at[GROUPS, 0])
    wg_store.start()

    og_send.wait_send()

    def drain(g, carry):
        store_q(g).wait()
        store_kv(g, 0).wait()
        store_kv(g, 1).wait()
        att_send(g).wait_send()
        for k in (1, 2, 3):
            z_send_a(g, k).wait_send()
            z_send_b(g, k).wait_send()
        x_send_a(g).wait_send()
        x_send_b(g).wait_send()

        @pl.when(g % 4 != y)
        def _():
            y_send(g).wait_send()

        for level in range(4):

            @pl.when(sends[level])
            def _():
                fwd(g, level).wait_send()

        @pl.when(hops_f)
        def _():
            fwd_hop(g).wait_send()

        @pl.when(jnp.logical_and(jnp.logical_and(c % 4 == 0, c <= 8), g < HOPS_B))
        def _():
            bwd_hop(g).wait_send()

        @pl.when(hands_on)
        def _():
            fwd_on(g).wait_send()
            bwd(g, 1).wait_send()

        @pl.when(c >= 1)
        def _():
            bwd(g, 0).wait_send()

        @pl.when(jnp.logical_and(odd, c >= 3))
        def _():
            bwd_relay(g).wait_send()

        @pl.when(c >= 4)
        def _():
            bwd(g, 2).wait_send()

        @pl.when(c >= 8)
        def _():
            bwd(g, 3).wait_send()

        return carry

    lax.fori_loop(0, GROUPS, drain, 0)
    x_send.wait_send()
    for k in range(1, NDP):
        share(k).wait_send()
    wg_store.wait()


def move_kernel(*refs):
    ins, outs, bufs, wide, sems = refs[:4], refs[4:8], refs[8:12], refs[12], refs[13]
    first, second = [], []
    for i in (3, 0, 1, 2):
        a, b = (ins[i].at[0], outs[i].at[0]) if i < 3 else (ins[i], outs[i])
        n = a.shape[0] // 2
        for j in range(2):
            rows = pl.ds(j * n, n)
            first.append(pltpu.make_async_copy(a.at[rows], bufs[i].at[rows], sems.at[0, i, j]))
            src = wide if i == 3 else bufs[i]
            second.append(pltpu.make_async_copy(src.at[rows], b.at[rows], sems.at[1, i, j]))
    for copy in first:
        copy.start()
    for at, (copy, then) in enumerate(zip(first, second)):
        copy.wait()
        if at < 2:
            rows = pl.ds(at * 64, 64)
            wide[rows] = bufs[3][rows].astype(F32)
        then.start()
    for copy in second:
        copy.wait()


def move_out(results):
    return pl.pallas_call(
        move_kernel,
        out_shape=tuple(jax.ShapeDtypeStruct(r.shape, r.dtype) for r in results[:3])
        + (jax.ShapeDtypeStruct(results[3].shape, F32),),
        in_specs=[pl.BlockSpec(memory_space=pl.ANY)] * 4,
        out_specs=(pl.BlockSpec(memory_space=pl.ANY),) * 4,
        scratch_shapes=[pltpu.VMEM(r.shape[-2:], r.dtype) for r in results]
        + [pltpu.VMEM(results[3].shape, F32), pltpu.SemaphoreType.DMA((2, 4, 2))],
        name="move_out",
    )(*results)


def per_device(query_in, key_in, value_in, out_grad, out_weight):
    vm = pltpu.VMEM
    dma = pltpu.SemaphoreType.DMA
    g = GROUPS
    results = pl.pallas_call(
        kernel,
        out_shape=(
            jax.ShapeDtypeStruct((1, TOK, 2048), BF16),
            jax.ShapeDtypeStruct((1, TOK, 2048), BF16),
            jax.ShapeDtypeStruct((1, TOK, 2048), BF16),
            jax.ShapeDtypeStruct((128, 2048), BF16),
        ),
        in_specs=[pl.BlockSpec(memory_space=pl.ANY)] * 5,
        out_specs=(pl.BlockSpec(memory_space=pl.ANY),) * 4,
        scratch_shapes=[
            vm((g, TOK, GW), BF16),
            vm((g, TOK, 2 * GW), BF16),
            vm((2, TOK, 2048), BF16),
            vm((g, GW, 2048), BF16),
            vm((g, KEYS, 2 * GW), BF16),
            vm((g, 480, 2 * GW), BF16),
            vm((g, 128, 2 * GW), BF16),
            vm((g, 480, 2 * GW), BF16),
            vm((g, TOK, 2 * GW), F32),
            vm((g, TOK, 2 * GW), BF16),
            vm((HOPS_B, TOK, 2 * GW), BF16),
            vm((g, HEAD, TOK), BF16),
            vm((g, HEAD, TOK), BF16),
            vm((g, HEAD, TOK), BF16),
            vm((g, 4, HEAD, 256), BF16),
            vm((g, 2, 4, HEAD, 128), BF16),
            vm((g, 3, HEAD, 256), BF16),
            vm((g, HEAD, 128), F32),
            vm((g, HEAD, 128), BF16),
            vm((g, HEAD, 128), BF16),
            vm((g, 4, HEAD, 128), BF16),
            vm((g, 4, HEAD, 128), BF16),
            vm((g, 3, HEAD, 128), BF16),
            vm((g, HEAD, 256), BF16),
            vm((2, 3, HEAD, 256), BF16),
            vm((HEAD, 256), F32),
            vm((HEAD, 256), BF16),
            vm((HEAD, 256), BF16),
            vm((NDP, HEAD, 256), BF16),
            vm((g, TOK, GW), BF16),
            vm((g, TOK, 2 * GW), BF16),
            vm((HEAD, 2048), BF16),
            vm((KEYS, TOK), F32),
            vm((TOK, TOK), BF16),
            vm((TOK, TOK), BF16),
            dma((g + 1, 4)),
            dma((g, 5)),
            dma((g, 5)),
            dma((g, 6)),
            dma((g, 6)),
            dma((g,)),
            dma((g,)),
            dma((2,)),
            dma((g, 3)),
            dma((g, 3)),
            dma((g, 3)),
            dma((g, 3)),
            dma((g, 2)),
            dma((g, 2)),
            dma((g,)),
            dma((2, 3)),
            dma((2,)),
            dma((NDP - 1,)),
            dma((NDP - 1,)),
            dma((g + 1, 3)),
        ],
        compiler_params=pltpu.CompilerParams(
            collective_id=0, has_side_effects=True, vmem_limit_bytes=60 * 2**20
        ),
        name="logsparse_backward",
    )(query_in, key_in, value_in, out_grad, out_weight)
    return move_out(results)


def solution(mesh):
    return jax.shard_map(
        per_device,
        mesh=mesh,
        in_specs=(
            P("dp", "seq", None),
            P("dp", "seq", None),
            P("dp", "seq", None),
            P("dp", "seq", None),
            P(),
        ),
        out_specs=(
            P("dp", "seq", None),
            P("dp", "seq", None),
            P("dp", "seq", None),
            P("seq", None),
        ),
        check_vma=False,
    )
```
